256 devices in a mesh: tm: 32 (over z, x), coef: 8 (over y, core).
Axes of the slice: x: 4, y: 4, z: 8, core: 2. Of those that a mesh axis runs over, the one named last changes fastest.
Arguments:
- design: float32 [24576, 16384], P('tm', 'coef'), may hold values from -6 to 6
- taps: float32 [384], replicated, may hold values from -0.3125 to 0.3125
Outputs:
- coeffs: float32 [256, 16384], P(None, 'coef')
- reduced: float32 [24576, 16384], P('tm', 'coef')
The draws below stay inside these ranges and needn't reach their ends.
All inputs are finite; a program needn't handle non-finite values.
Results may differ from the reference program's by a relative error of at most 0.0003.
Values sent between devices are 32-bit elements; how exact they have to be, the bound alone decides.
A program may use at most 64 MiB of HBM per device.

```python
import jax
import jax.numpy as jnp
from jax import lax

COLS = 16384
TAPS = 384
PANEL = 256
ROWS_DEV = 768
TIME = 24576
N_TM = 32


def steps_of(stream_key, dims, shards, low, top_value):
    factor_of = 1.0
    for axis_at, parts in shards:
        steps = jax.random.uniform(jax.random.fold_in(jax.random.fold_in(stream_key, 6), axis_at), (parts,), jnp.float32, low / len(shards), top_value / len(shards))
        factor_of = factor_of * jnp.repeat(jnp.exp(steps), dims[axis_at] // parts).reshape((-1,) + (1,) * (len(dims) - 1 - axis_at))
    return factor_of


def normal_values(key, dims, spread, limit, split=(), kind=jnp.bfloat16):
    entries = jax.random.normal(key, dims, jnp.float32) * spread
    if len(split) > 0:
        entries = steps_of(key, dims, split, -0.22, 0.18) * entries
    return jnp.clip(entries, min=-limit, max=limit).astype(kind)


def setup_inputs(seed: int = 0) -> dict:
    arg_keys = jax.random.split(jax.random.key(seed), 3)
    return {
        "design": normal_values(arg_keys[0], (TIME, COLS), 1.0, 6.0, ((0, 32), (1, 8)), jnp.float32),
        "taps": normal_values(arg_keys[1], (TAPS,), TAPS ** -0.5, 0.3125, (), jnp.float32),
    }


def solve_lower(lower, right):
    return lax.linalg.triangular_solve(lower, right, left_side=True, lower=True)

def toeplitz_matrix(taps, height):
    count = taps.shape[0]
    span = height + count - 1
    pattern = jnp.concatenate([taps[::-1], jnp.zeros((span + 1 - count,), taps.dtype)])
    repeated = jnp.tile(pattern, height)
    return repeated[:height * span].reshape(height, span)

def reference(design, taps):
    extra = TAPS - 1
    matrix = toeplitz_matrix(taps, ROWS_DEV)
    padded = jnp.concatenate([jnp.zeros((extra, COLS), jnp.float32), design], axis=0)

    def block(index):
        start = (index * ROWS_DEV).astype(jnp.int32)
        rows = lax.dynamic_slice_in_dim(padded, start, ROWS_DEV + extra, 0)
        return jnp.dot(matrix.astype(jnp.float32), rows.astype(jnp.float32), precision=lax.Precision.HIGHEST, preferred_element_type=jnp.float32)
    white = lax.map(block, jnp.arange(N_TM, dtype=jnp.int32)).reshape(TIME, COLS)
    panel = white[:, :PANEL]
    gram = jnp.dot(panel.T.astype(jnp.float32), panel.astype(jnp.float32), precision=lax.Precision.HIGHEST, preferred_element_type=jnp.float32)
    lower = jnp.linalg.cholesky(gram)
    cross = jnp.dot(panel.T.astype(jnp.float32), white.astype(jnp.float32), precision=lax.Precision.HIGHEST, preferred_element_type=jnp.float32)
    coeffs = solve_lower(lower, cross)
    basis = solve_lower(lower, panel.T).T
    reduced = white - jnp.dot(basis.astype(jnp.float32), coeffs.astype(jnp.float32), precision=lax.Precision.HIGHEST, preferred_element_type=jnp.float32)
    reduced = reduced.at[:, :PANEL].set(jnp.sqrt(jnp.float32(TIME)) * basis)
    return (coeffs, reduced)
```

```python
import functools

import jax
import jax.numpy as jnp
from jax import lax
from jax.experimental import pallas as pl
from jax.experimental.pallas import tpu as pltpu
from jax.sharding import PartitionSpec as P

MESH = pl.DeviceIdType.MESH
F32 = jnp.float32
BF16 = jnp.bfloat16
HIGHEST = lax.Precision.HIGHEST
PANEL = 256
ROWS = 768
REACH = 384
COLUMNS = 2048
CHUNK = 256
CHUNKS = COLUMNS // CHUNK
TILE = 128
NX = 4
PIECES = 8
PIECE_ROWS = 192
PIECE_ORDER = (2, 3, 4, 5, 0, 1, 6, 7)
PLUS = 3
MINUS = 4
SUBS = 2
SUB_ROWS = PANEL // SUBS


def split(value):
    high = value.astype(BF16)
    low = (value - high.astype(F32)).astype(BF16)
    return high, low


def dot(left, right):
    return jnp.dot(left, right, preferred_element_type=F32)


def exact(left, right):
    return jnp.dot(left, right, precision=HIGHEST, preferred_element_type=F32)


def stacked_product(stacked, high, low):
    rows = stacked.shape[0] // 2
    both = dot(stacked, high)
    return both[:rows] + (both[rows:] + dot(stacked[:rows], low))


def build_bands(taps_ref, ahead, behind, behind_split):
    line = jnp.concatenate([taps_ref[...], jnp.zeros((1, TILE), F32)], axis=1)
    band = jnp.broadcast_to(line, (TILE, 4 * TILE))
    row = lax.broadcasted_iota(jnp.int32, (TILE, 4 * TILE), 0)
    step = 1
    while step < TILE:
        band = jnp.where((row // step) % 2 == 1, pltpu.roll(band, step, 1), band)
        step *= 2
    ahead[...] = band
    for block in range(4):
        part = band[:, (3 - block) * TILE : (4 - block) * TILE].T
        columns = slice(block * TILE, (block + 1) * TILE)
        behind[:, columns] = part
        high, low = split(part)
        behind_split[:TILE, columns] = high
        behind_split[TILE:, columns] = low


def eliminate(work, block):
    size = 64
    top = block * size
    rows = slice(top, top + size)
    square = work[rows, top : top + size]
    eye_row = lax.broadcasted_iota(jnp.int32, (size, size), 0)
    eye_column = lax.broadcasted_iota(jnp.int32, (size, size), 1)
    eye = jnp.where(eye_row == eye_column, 1.0, 0.0).astype(F32)
    table = jnp.concatenate([square, eye], axis=1)
    row = lax.broadcasted_iota(jnp.int32, (size, 2 * size), 0)
    for j in range(size):
        column = jnp.broadcast_to(table[:, j : j + 1], (size, 2 * size))
        inverse_root = lax.rsqrt(column[j : j + 1, :])
        pivot = table[j : j + 1, :] * inverse_root
        factor = column * inverse_root
        table = jnp.where(row == j, pivot, jnp.where(row > j, table - factor * pivot, table))
    inverse = table[:, size:]
    panel_rows = exact(inverse, work[rows, :])
    work[rows, :] = panel_rows
    if top + size < PANEL:
        left = panel_rows[:, :PANEL].T[top + size :]
        rest = slice(top + size, PANEL)
        work[rest, :] = work[rest, :] - exact(left, panel_rows)


def exchange_kernel(
    nz, ny, taps_ref, design, white, coeffs, basis,
    slab, halo, wide, panel, cross_left, ahead, behind, behind_split, crossed,
    from_minus, from_plus, across, gathered, gram_own, gram_in, gram_x, gram_all, work,
    load_sem, halo_send, halo_recv, side_send, side_recv, own_sem,
    flow_send, flow_recv, core_send, core_recv,
    gz_send, gz_recv, gx_send, gx_recv, ga_send, ga_recv, gc_send, gc_recv,
    rp_send, rp_recv, rm_send, rm_recv, xs_send, xs_recv, xg_send, xg_recv,
    ap_send, ap_recv, am_send, am_recv,
):
    tm = lax.axis_index("tm")
    coef = lax.axis_index("coef")
    last_tm = nz * NX - 1
    z, x = tm // NX, tm % NX
    y, core = coef // 2, coef % 2
    is_source = coef == 0

    def at(z_to=z, x_to=x, coef_to=coef):
        return (z_to * NX + x_to, coef_to)

    def send(source, target, send_sem, recv_sem, device):
        return pltpu.make_async_remote_copy(
            src_ref=source, dst_ref=target, send_sem=send_sem, recv_sem=recv_sem,
            device_id=device, device_id_type=MESH,
        )

    wrap_up = (x == NX - 1) & (tm < last_tm)
    wrap_down = (x == 0) & (tm > 0)

    for q in range(CHUNKS):
        pltpu.make_async_copy(
            design.at[:, pl.ds(q * CHUNK, CHUNK)], slab.at[q], load_sem.at[q]
        ).start()

    barrier = pltpu.get_barrier_semaphore()

    def greet(device):
        pl.semaphore_signal(barrier, inc=1, device_id=device, device_id_type=MESH)

    for d in range(1, nz):
        greet(at(z_to=(z + d) % nz))
    for d in range(1, NX):
        greet(at(x_to=(x + d) % NX))
    for d in range(1, 2 * ny):
        greet(at(coef_to=(coef + d) % (2 * ny)))
    greetings = nz - 1 + NX - 1 + 2 * ny - 1

    @pl.when(wrap_up)
    def _():
        greet((tm + 1, coef))

    @pl.when(wrap_down)
    def _():
        greet((tm - 1, coef))

    extra = jnp.where(wrap_up, 1, 0) + jnp.where(wrap_down, 1, 0)
    pl.semaphore_wait(barrier, greetings + extra)

    def side(direction, half):
        lanes = pl.ds(half * TILE, TILE)
        if direction == 0:
            source, device, start = design.at[pl.ds(ROWS - REACH, REACH), lanes], (tm + 1, coef), 0
        else:
            source, device, start = design.at[pl.ds(0, REACH), lanes], (tm - 1, coef), REACH + ROWS
        target = wide.at[half, pl.ds(start, REACH), :]
        return send(source, target, side_send.at[direction, half], side_recv.at[direction, half], device)

    def own(half):
        return pltpu.make_async_copy(
            design.at[:, pl.ds(half * TILE, TILE)],
            wide.at[half, pl.ds(REACH, ROWS), :],
            own_sem.at[half],
        )

    def halo_copy(q):
        return send(
            design.at[pl.ds(ROWS - REACH, REACH), pl.ds(q * CHUNK, CHUNK)],
            halo.at[q], halo_send.at[q], halo_recv.at[q], (tm + 1, coef),
        )

    @pl.when(is_source)
    def _():
        for half in range(2):
            own(half).start()

        @pl.when(tm < last_tm)
        def _():
            for half in range(2):
                side(0, half).start()

        @pl.when(tm > 0)
        def _():
            for half in range(2):
                side(1, half).start()

        @pl.when(tm == 0)
        def _():
            wide[:, :REACH, :] = jnp.zeros((2, REACH, TILE), F32)

        @pl.when(tm == last_tm)
        def _():
            wide[:, REACH + ROWS :, :] = jnp.zeros((2, REACH, TILE), F32)

    @pl.when(tm < last_tm)
    def _():
        for q in range(CHUNKS):
            halo_copy(q).start()

    @pl.when(tm == 0)
    def _():
        for q in range(CHUNKS):
            halo[q] = jnp.zeros((REACH, CHUNK), F32)

    build_bands(taps_ref, ahead, behind, behind_split)

    def filtered(block):
        high, low = split(block)
        parts = []
        for i in range(3):
            window = slice(i * TILE, i * TILE + 4 * TILE)
            parts.append(stacked_product(behind_split[...], high[window], low[window]))
        return jnp.concatenate(parts, axis=0)

    def late_rows(q):
        white[q, REACH:, :] = filtered(slab[q])

    def early_rows(q):
        @pl.when(tm > 0)
        def _():
            halo_copy(q).wait_recv()

        white[q, :REACH, :] = filtered(jnp.concatenate([halo[q], slab[q, :REACH, :]], axis=0))

    def piece(half, p):
        return wide.at[half, pl.ds(PIECE_ORDER[p] * PIECE_ROWS, PIECE_ROWS), :]

    def flow(half, p):
        y_to = (y + 1) % ny if half == 0 else (y + ny - 1) % ny
        return send(
            piece(half, p), piece(half, p), flow_send.at[half, p], flow_recv.at[half, p],
            at(coef_to=y_to * 2),
        )

    def to_core(half, p):
        return send(
            piece(half, p), piece(half, p), core_send.at[half, p], core_recv.at[half, p],
            at(coef_to=y * 2 + 1),
        )

    end_of = (ny - 1, 1)
    lag = 2
    for p in range(PIECES + lag):
        if p < PIECES:

            @pl.when(is_source)
            def _():
                if p == 0:
                    for half in range(2):
                        own(half).wait()
                if p == 4:

                    @pl.when(tm > 0)
                    def _():
                        for half in range(2):
                            side(0, half).wait_recv()

                if p == 6:

                    @pl.when(tm < last_tm)
                    def _():
                        for half in range(2):
                            side(1, half).wait_recv()

        for half in range(2):
            if p < PIECES:

                @pl.when((core == 0) & (y != end_of[half]))
                def _():
                    @pl.when(y != 0)
                    def _():
                        flow(half, p).wait_recv()

                    flow(half, p).start()
                    to_core(half, p).start()

            if p >= lag:

                @pl.when((core == 0) & (y == end_of[half]))
                def _():
                    flow(half, p - lag).wait_recv()
                    to_core(half, p - lag).start()

        if p < CHUNKS:
            pltpu.make_async_copy(
                design.at[:, pl.ds(p * CHUNK, CHUNK)], slab.at[p], load_sem.at[p]
            ).wait()
            late_rows(p)

    @pl.when(core == 1)
    def _():
        for p in range(PIECES):
            for half in range(2):
                to_core(half, p).wait_recv()

    def panel_tile(i):
        rows = pl.ds(i * TILE, 4 * TILE)
        window = jnp.concatenate([wide[0, rows, :], wide[1, rows, :]], axis=1)
        return exact(behind[...], window)

    for i in range(ROWS // TILE):
        panel[i * TILE : (i + 1) * TILE, :] = panel_tile(i)
    own_panel = panel[:ROWS, :]
    work[:, :PANEL] = exact(own_panel.T, own_panel)
    for j in range(nz):
        rows = pl.ds(pl.multiple_of(coef * 32 + (j // 2) * 8, 8), 8)
        gram_own[j] = work[rows, (j % 2) * TILE : (j % 2 + 1) * TILE]

    def gram_scatter(d):
        return send(
            gram_own.at[(z + d) % nz], gram_in.at[z], gz_send.at[d], gz_recv.at[z],
            at(z_to=(z + d) % nz),
        )

    def gram_scatter_in(d):
        peer = (z + d) % nz
        return send(gram_own.at[peer], gram_in.at[peer], gz_send.at[d], gz_recv.at[peer], at(z_to=peer))

    def gram_across(d):
        return send(gram_x.at[x], gram_x.at[x], gx_send.at[d], gx_recv.at[x], at(x_to=(x + d) % NX))

    def gram_across_in(d):
        peer = (x + d) % NX
        return send(gram_x.at[peer], gram_x.at[peer], gx_send.at[d], gx_recv.at[peer], at(x_to=peer))

    def gram_gather(d):
        part = gram_all.at[coef, z]
        return send(part, part, ga_send.at[d], ga_recv.at[z], at(z_to=(z + d) % nz))

    def gram_gather_in(d):
        peer = (z + d) % nz
        part = gram_all.at[coef, peer]
        return send(part, part, ga_send.at[d], ga_recv.at[peer], at(z_to=peer))

    def gram_spread(d):
        part = gram_all.at[coef]
        return send(part, part, gc_send.at[d], gc_recv.at[coef], at(coef_to=(coef + d) % (2 * ny)))

    def gram_spread_in(d):
        peer = (coef + d) % (2 * ny)
        part = gram_all.at[peer]
        return send(part, part, gc_send.at[d], gc_recv.at[peer], at(coef_to=peer))

    for d in range(1, nz):
        gram_scatter(d).start()

    for i in range(ROWS // TILE, (ROWS + REACH) // TILE):
        panel[i * TILE : (i + 1) * TILE, :] = jnp.where(tm == last_tm, 0.0, panel_tile(i))
    for i in range(ROWS // TILE):
        columns = slice(i * TILE, (i + 1) * TILE)
        tile = exact(ahead[...], panel[i * TILE : i * TILE + 4 * TILE, :])
        high, low = split(tile.T)
        cross_left[:PANEL, columns] = high
        cross_left[PANEL:, columns] = low

    def cross_chunk(q):
        high, low = split(slab[q])
        crossed[q] = stacked_product(cross_left[...], high, low)

    def sub(s):
        return pl.ds(s * SUB_ROWS, SUB_ROWS)

    def up_index(step):
        return (z + PLUS - step) % nz

    def down_index(step):
        return (z + nz - MINUS + step) % nz

    def reduce_up(step, s):
        return send(
            crossed.at[up_index(step), sub(s), :], from_minus.at[step, sub(s), :],
            rp_send.at[step, s], rp_recv.at[step, s], at(z_to=(z + 1) % nz),
        )

    def reduce_down(step, s):
        return send(
            crossed.at[down_index(step), sub(s), :], from_plus.at[step, sub(s), :],
            rm_send.at[step, s], rm_recv.at[step, s], at(z_to=(z + nz - 1) % nz),
        )

    def start_sums(kind):
        for s in range(SUBS):
            kind(0, s).start()

    def pass_up(step):
        for s in range(SUBS):
            reduce_up(step - 1, s).wait_recv()
            index = up_index(step)
            crossed[index, sub(s), :] = crossed[index, sub(s), :] + from_minus[step - 1, sub(s), :]
            if step < PLUS:
                reduce_up(step, s).start()

    def pass_down(step):
        for s in range(SUBS):
            reduce_down(step - 1, s).wait_recv()
            index = down_index(step)
            crossed[index, sub(s), :] = crossed[index, sub(s), :] + from_plus[step - 1, sub(s), :]
            if step < MINUS:
                reduce_down(step, s).start()

    cross_chunk(down_index(0))
    start_sums(reduce_down)
    cross_chunk(up_index(0))
    start_sums(reduce_up)

    total = gram_own[z]
    for d in range(1, nz):
        gram_scatter_in(d).wait_recv()
        total = total + gram_in[(z + d) % nz]
    gram_x[x] = total
    for d in range(1, NX):
        gram_across(d).start()
    cross_chunk(down_index(1))
    cross_chunk(up_index(1))
    for d in range(1, NX):
        gram_across_in(d).wait_recv()
    total = gram_x[0]
    for i in range(1, NX):
        total = total + gram_x[i]
    gram_all[coef, z] = total
    for d in range(1, nz):
        gram_gather(d).start()
    cross_chunk(down_index(2))
    cross_chunk(up_index(2))
    for d in range(1, nz):
        gram_gather_in(d).wait_recv()
    for d in range(1, 2 * ny):
        gram_spread(d).start()
    cross_chunk(down_index(3))
    cross_chunk(z)
    for d in range(1, 2 * ny):
        gram_spread_in(d).wait_recv()
    for c in range(2 * ny):
        for j in range(nz):
            top = c * 32 + (j // 2) * 8
            work[top : top + 8, (j % 2) * TILE : (j % 2 + 1) * TILE] = gram_all[c, j]
    eye_row = lax.broadcasted_iota(jnp.int32, (PANEL, PANEL), 0)
    eye_column = lax.broadcasted_iota(jnp.int32, (PANEL, PANEL), 1)
    work[:, PANEL:] = jnp.where(eye_row == eye_column, 1.0, 0.0).astype(F32)

    pass_down(1)
    pass_up(1)
    eliminate(work, 0)
    pass_down(2)
    pass_up(2)
    eliminate(work, 1)
    pass_down(3)
    pass_up(3)
    eliminate(work, 2)
    pass_down(4)

    quarter = PANEL // NX

    def x_rows(index):
        return pl.ds(pl.multiple_of(index * quarter, quarter), quarter)

    def across_out(d):
        peer = (x + d) % NX
        return send(
            crossed.at[z, x_rows(peer), :], across.at[x], xs_send.at[d], xs_recv.at[x],
            at(x_to=peer),
        )

    def across_in(d):
        peer = (x + d) % NX
        return send(
            crossed.at[z, x_rows(peer), :], across.at[peer], xs_send.at[d], xs_recv.at[peer],
            at(x_to=peer),
        )

    def gather_out(d):
        part = gathered.at[x_rows(x), :]
        return send(part, part, xg_send.at[d], xg_recv.at[x], at(x_to=(x + d) % NX))

    def gather_in(d):
        peer = (x + d) % NX
        part = gathered.at[x_rows(peer), :]
        return send(part, part, xg_send.at[d], xg_recv.at[peer], at(x_to=peer))

    for d in range(1, NX):
        across_out(d).start()
    eliminate(work, 3)
    total = crossed[z, x_rows(x), :]
    for d in range(1, NX):
        across_in(d).wait_recv()
        total = total + across[(x + d) % NX]
    gathered[x_rows(x), :] = total
    for d in range(1, NX):
        gather_out(d).start()
    basis[...] = exact(panel[:ROWS, :], work[:, PANEL:].T)
    for d in range(1, NX):
        gather_in(d).wait_recv()
    coeffs[z] = exact(work[:, PANEL:], gathered[...])

    def ring_up(step, s):
        part = coeffs.at[(z + nz - step) % nz, sub(s), :]
        return send(part, part, ap_send.at[step, s], ap_recv.at[step, s], at(z_to=(z + 1) % nz))

    def ring_up_in(step, s):
        part = coeffs.at[(z + nz - step) % nz, sub(s), :]
        return send(part, part, ap_send.at[step - 1, s], ap_recv.at[step - 1, s], at(z_to=(z + 1) % nz))

    def ring_down(step, s):
        part = coeffs.at[(z + step) % nz, sub(s), :]
        return send(part, part, am_send.at[step, s], am_recv.at[step, s], at(z_to=(z + nz - 1) % nz))

    def ring_down_in(step, s):
        part = coeffs.at[(z + step) % nz, sub(s), :]
        return send(part, part, am_send.at[step - 1, s], am_recv.at[step - 1, s], at(z_to=(z + 1) % nz))

    up_hops, down_hops = PLUS, MINUS
    for s in range(SUBS):
        ring_up(0, s).start()
        ring_down(0, s).start()
    early_rows(0)
    for step in range(1, max(up_hops, down_hops) + 1):
        for s in range(SUBS):
            if step <= up_hops:
                ring_up_in(step, s).wait_recv()
                if step < up_hops:
                    ring_up(step, s).start()
            if step <= down_hops:
                ring_down_in(step, s).wait_recv()
                if step < down_hops:
                    ring_down(step, s).start()
        for q in range(2 * step - 1, min(2 * step + 1, CHUNKS)):
            early_rows(q)

    @pl.when(tm < last_tm)
    def _():
        for q in range(CHUNKS):
            halo_copy(q).wait_send()

    @pl.when(is_source)
    def _():
        @pl.when(tm < last_tm)
        def _():
            for half in range(2):
                side(0, half).wait_send()

        @pl.when(tm > 0)
        def _():
            for half in range(2):
                side(1, half).wait_send()

    @pl.when(core == 0)
    def _():
        for half in range(2):
            for p in range(PIECES):
                to_core(half, p).wait_send()

            @pl.when(y != end_of[half])
            def _():
                for p in range(PIECES):
                    flow(half, p).wait_send()

    for d in range(1, nz):
        gram_scatter(d).wait_send()
        gram_gather(d).wait_send()
    for d in range(1, NX):
        gram_across(d).wait_send()
        across_out(d).wait_send()
        gather_out(d).wait_send()
    for d in range(1, 2 * ny):
        gram_spread(d).wait_send()
    for s in range(SUBS):
        for step in range(PLUS):
            reduce_up(step, s).wait_send()
        for step in range(MINUS):
            reduce_down(step, s).wait_send()
        for step in range(up_hops):
            ring_up(step, s).wait_send()
        for step in range(down_hops):
            ring_down(step, s).wait_send()


def finish_kernel(scale, white, coeffs, basis, coeffs_out, reduced_out, high, low):
    q = pl.program_id(0)

    @pl.when(q == 0)
    def _():
        top, rest = split(basis[...])
        high[...] = top
        low[...] = rest

    chunk = coeffs[q]
    coeffs_out[...] = chunk
    top, rest = split(chunk)
    product = dot(high[...], top) + (dot(high[...], rest) + dot(low[...], top))
    reduced_out[...] = white[q] - product

    @pl.when((q == 0) & (lax.axis_index("coef") == 0))
    def _():
        reduced_out[...] = basis[...] * scale


def per_device(nz, ny, design, taps):
    dma = pltpu.SemaphoreType.DMA
    vmem = pltpu.VMEM
    white, coeffs, basis = pl.pallas_call(
        functools.partial(exchange_kernel, nz, ny),
        out_shape=(
            vmem((CHUNKS, ROWS, CHUNK), F32),
            vmem((CHUNKS, PANEL, CHUNK), F32),
            vmem((ROWS, PANEL), F32),
        ),
        in_specs=[pl.BlockSpec(memory_space=pltpu.VMEM), pl.BlockSpec(memory_space=pl.ANY)],
        out_specs=[pl.BlockSpec(memory_space=pltpu.VMEM)] * 3,
        scratch_shapes=[
            vmem((CHUNKS, ROWS, CHUNK), F32),
            vmem((CHUNKS, REACH, CHUNK), F32),
            vmem((2, 2 * REACH + ROWS, TILE), F32),
            vmem((ROWS + REACH, PANEL), F32),
            vmem((2 * PANEL, ROWS), BF16),
            vmem((TILE, 4 * TILE), F32),
            vmem((TILE, 4 * TILE), F32),
            vmem((2 * TILE, 4 * TILE), BF16),
            vmem((CHUNKS, PANEL, CHUNK), F32),
            vmem((PLUS, PANEL, CHUNK), F32),
            vmem((MINUS, PANEL, CHUNK), F32),
            vmem((NX, PANEL // NX, CHUNK), F32),
            vmem((PANEL, CHUNK), F32),
            vmem((nz, 8, TILE), F32),
            vmem((nz, 8, TILE), F32),
            vmem((NX, 8, TILE), F32),
            vmem((2 * ny, nz, 8, TILE), F32),
            vmem((PANEL, 2 * PANEL), F32),
            dma((CHUNKS,)), dma((CHUNKS,)), dma((CHUNKS,)),
            dma((2, 2)), dma((2, 2)), dma((2,)),
            dma((2, PIECES)), dma((2, PIECES)), dma((2, PIECES)), dma((2, PIECES)),
            dma((nz,)), dma((nz,)), dma((NX,)), dma((NX,)),
            dma((nz,)), dma((nz,)), dma((2 * ny,)), dma((2 * ny,)),
            dma((PLUS, SUBS)), dma((PLUS, SUBS)), dma((MINUS, SUBS)), dma((MINUS, SUBS)),
            dma((NX,)), dma((NX,)), dma((NX,)), dma((NX,)),
            dma((PLUS, SUBS)), dma((PLUS, SUBS)), dma((MINUS, SUBS)), dma((MINUS, SUBS)),
        ],
        compiler_params=pltpu.CompilerParams(
            collective_id=0, has_side_effects=True, vmem_limit_bytes=40 * 1024 * 1024
        ),
    )(taps.reshape(1, -1), design)
    scale = float((nz * NX * ROWS) ** 0.5)
    keep = pltpu.with_memory_space_constraint
    return pl.pallas_call(
        functools.partial(finish_kernel, scale),
        grid=(CHUNKS,),
        out_shape=(
            jax.ShapeDtypeStruct((PANEL, COLUMNS), F32),
            jax.ShapeDtypeStruct((ROWS, COLUMNS), F32),
        ),
        in_specs=[pl.BlockSpec(memory_space=pltpu.VMEM)] * 3,
        out_specs=[
            pl.BlockSpec((PANEL, CHUNK), lambda q: (0, q)),
            pl.BlockSpec((ROWS, CHUNK), lambda q: (0, q)),
        ],
        scratch_shapes=[vmem((ROWS, PANEL), BF16), vmem((ROWS, PANEL), BF16)],
        compiler_params=pltpu.CompilerParams(vmem_limit_bytes=24 * 1024 * 1024),
    )(keep(white, pltpu.VMEM), keep(coeffs, pltpu.VMEM), keep(basis, pltpu.VMEM))


def solution(mesh):
    nz = mesh.shape["tm"] // NX
    ny = mesh.shape["coef"] // 2
    in_specs = (P("tm", "coef"), P())
    out_specs = (P(None, "coef"), P("tm", "coef"))
    return jax.shard_map(
        functools.partial(per_device, nz, ny), mesh=mesh, in_specs=in_specs,
        out_specs=out_specs, check_vma=False,
    )
```

```python
import functools

import jax
import jax.numpy as jnp
from jax import lax
from jax.experimental import pallas as pl
from jax.experimental.pallas import tpu as pltpu
from jax.sharding import PartitionSpec as P

MESH = pl.DeviceIdType.MESH
F32 = jnp.float32
BF16 = jnp.bfloat16
HIGHEST = lax.Precision.HIGHEST
PANEL = 256
ROWS = 768
REACH = 384
COLUMNS = 2048
CHUNK = 256
CHUNKS = COLUMNS // CHUNK
TILE = 128
NX = 4
PIECES = 8
PIECE_ROWS = 192
PIECE_ORDER = (2, 3, 4, 5, 0, 6, 1, 7)
PLUS = 3
MINUS = 4
SUBS = 2
SUB_ROWS = PANEL // SUBS
FIRST, LAST = (0, 1, 2, 3, 4, 5), (6, 7)
RELAYED = (3, 4, 5, 7)


def split(value):
    high = value.astype(BF16)
    low = (value - high.astype(F32)).astype(BF16)
    return high, low


def dot(left, right):
    return jnp.dot(left, right, preferred_element_type=F32)


def exact(left, right):
    return jnp.dot(left, right, precision=HIGHEST, preferred_element_type=F32)


def stacked_product(stacked, high, low):
    rows = stacked.shape[0] // 2
    both = dot(stacked, high)
    return both[:rows] + (both[rows:] + dot(stacked[:rows], low))


def build_bands(taps_ref, ahead, behind, behind_split):
    line = jnp.concatenate([taps_ref[...], jnp.zeros((1, TILE), F32)], axis=1)
    band = jnp.broadcast_to(line, (TILE, 4 * TILE))
    row = lax.broadcasted_iota(jnp.int32, (TILE, 4 * TILE), 0)
    step = 1
    while step < TILE:
        band = jnp.where((row // step) % 2 == 1, pltpu.roll(band, step, 1), band)
        step *= 2
    ahead[...] = band
    for block in range(4):
        part = band[:, (3 - block) * TILE : (4 - block) * TILE].T
        columns = slice(block * TILE, (block + 1) * TILE)
        behind[:, columns] = part
        high, low = split(part)
        behind_split[:TILE, columns] = high
        behind_split[TILE:, columns] = low


def eliminate(work, block):
    size = 64
    top = block * size
    rows = slice(top, top + size)
    square = work[rows, top : top + size]
    eye_row = lax.broadcasted_iota(jnp.int32, (size, size), 0)
    eye_column = lax.broadcasted_iota(jnp.int32, (size, size), 1)
    eye = jnp.where(eye_row == eye_column, 1.0, 0.0).astype(F32)
    table = jnp.concatenate([square, eye], axis=1)
    row = lax.broadcasted_iota(jnp.int32, (size, 2 * size), 0)
    for j in range(size):
        column = jnp.broadcast_to(table[:, j : j + 1], (size, 2 * size))
        inverse_root = lax.rsqrt(column[j : j + 1, :])
        pivot = table[j : j + 1, :] * inverse_root
        factor = column * inverse_root
        table = jnp.where(row == j, pivot, jnp.where(row > j, table - factor * pivot, table))
    inverse = table[:, size:]
    panel_rows = exact(inverse, work[rows, :])
    work[rows, :] = panel_rows
    if top + size < PANEL:
        left = panel_rows[:, :PANEL].T[top + size :]
        rest = slice(top + size, PANEL)
        work[rest, :] = work[rest, :] - exact(left, panel_rows)


def exchange_kernel(
    nz, ny, taps_ref, design, white, coeffs,
    basis, basis_split, slab, halo, relay, wide, panel, cross_left, ahead, behind, behind_split, crossed,
    from_minus, from_plus, across, gathered, gram_own, gram_in, gram_x, gram_all, work,
    load_sem, halo_send, halo_recv, relay_send, relay_recv, side_send, side_recv, own_sem,
    flow_send, flow_recv, core_send, core_recv,
    gz_send, gz_recv, gx_send, gx_recv, ga_send, ga_recv, gc_send, gc_recv,
    rp_send, rp_recv, rm_send, rm_recv, xs_send, xs_recv, xg_send, xg_recv,
    ap_send, ap_recv, am_send, am_recv,
):
    tm = lax.axis_index("tm")
    coef = lax.axis_index("coef")
    last_tm = nz * NX - 1
    z, x = tm // NX, tm % NX
    y, core = coef // 2, coef % 2
    is_source = coef == 0

    def at(z_to=z, x_to=x, coef_to=coef):
        return (z_to * NX + x_to, coef_to)

    def send(source, target, send_sem, recv_sem, device):
        return pltpu.make_async_remote_copy(
            src_ref=source, dst_ref=target, send_sem=send_sem, recv_sem=recv_sem,
            device_id=device, device_id_type=MESH,
        )

    wrap_up = (x == NX - 1) & (tm < last_tm)
    wrap_down = (x == 0) & (tm > 0)

    def own(half):
        return pltpu.make_async_copy(
            design.at[:, pl.ds(half * TILE, TILE)],
            wide.at[half, pl.ds(REACH, ROWS), :],
            own_sem.at[half],
        )

    @pl.when(is_source)
    def _():
        for half in range(2):
            own(half).start()

    for q in range(CHUNKS):
        pltpu.make_async_copy(
            design.at[:, pl.ds(q * CHUNK, CHUNK)], slab.at[q], load_sem.at[q]
        ).start()

    barrier = pltpu.get_barrier_semaphore()

    def greet(device):
        pl.semaphore_signal(barrier, inc=1, device_id=device, device_id_type=MESH)

    for d in range(1, nz):
        greet(at(z_to=(z + d) % nz))
    for d in range(1, NX):
        greet(at(x_to=(x + d) % NX))
    for d in range(1, 2 * ny):
        greet(at(coef_to=(coef + d) % (2 * ny)))
    greetings = nz - 1 + NX - 1 + 2 * ny - 1

    @pl.when(wrap_up)
    def _():
        greet((tm + 1, coef))

    @pl.when(wrap_down)
    def _():
        greet((tm - 1, coef))

    extra = jnp.where(wrap_up, 1, 0) + jnp.where(wrap_down, 1, 0)
    pl.semaphore_wait(barrier, greetings + extra)

    def side(direction, half, part):
        skip = part * PIECE_ROWS
        if direction == 0:
            source = wide.at[half, pl.ds(ROWS + skip, PIECE_ROWS), :]
            device, start = (tm + 1, coef), skip
        else:
            source = wide.at[half, pl.ds(REACH + skip, PIECE_ROWS), :]
            device, start = (tm - 1, coef), REACH + ROWS + skip
        target = wide.at[half, pl.ds(start, PIECE_ROWS), :]
        sems = side_send.at[direction, half, part], side_recv.at[direction, half, part]
        return send(source, target, *sems, device)

    def halo_source(q):
        return slab.at[q, pl.ds(ROWS - REACH, REACH), :]

    def halo_copy(q):
        sems = halo_send.at[q], halo_recv.at[q]
        return send(halo_source(q), halo.at[q], *sems, (tm + 1, coef))

    def relay_out(q):
        i = RELAYED.index(q)
        sems = relay_send.at[0, i], relay_recv.at[i]
        return send(halo_source(q), relay.at[i], *sems, at(z_to=(z + 1) % nz))

    def relay_on(q):
        i = RELAYED.index(q)
        sems = relay_send.at[1, i], halo_recv.at[q]
        return send(relay.at[i], halo.at[q], *sems, at(x_to=(x + 1) % NX))

    wrap_relay = (x == NX - 1) & (z > 0)

    def start_halo(group, direct, relayed, passed):
        if group:

            @pl.when(x < NX - 1)
            def _():
                for q in group:
                    halo_copy(q).start()

        if relayed:

            @pl.when(wrap_up)
            def _():
                for q in relayed:
                    relay_out(q).start()

        if direct or passed:

            @pl.when(x == NX - 1)
            def _():
                for q in sorted(direct + passed):
                    if q in passed:

                        @pl.when(z > 0)
                        def _():
                            relay_out(q).wait_recv()
                            relay_on(q).start()

                    else:

                        @pl.when(tm < last_tm)
                        def _():
                            halo_copy(q).start()

    @pl.when(is_source)
    def _():
        for half in range(2):
            own(half).wait()

        @pl.when(tm < last_tm)
        def _():
            for part in range(2):
                for half in range(2):
                    side(0, half, part).start()

        @pl.when(tm > 0)
        def _():
            for part in range(2):
                for half in range(2):
                    side(1, half, part).start()

        @pl.when(tm == 0)
        def _():
            wide[:, :REACH, :] = jnp.zeros((2, REACH, TILE), F32)

        @pl.when(tm == last_tm)
        def _():
            wide[:, REACH + ROWS :, :] = jnp.zeros((2, REACH, TILE), F32)

    @pl.when(tm == 0)
    def _():
        for q in range(CHUNKS):
            halo[q] = jnp.zeros((REACH, CHUNK), F32)

    def filtered(block):
        high, low = split(block)
        parts = []
        for i in range(3):
            window = slice(i * TILE, i * TILE + 4 * TILE)
            parts.append(stacked_product(behind_split[...], high[window], low[window]))
        return jnp.concatenate(parts, axis=0)

    def late_rows(q):
        white[q, REACH:, :] = filtered(slab[q])
        white[q, :REACH, :] = jnp.zeros((REACH, CHUNK), F32)

    def late_range(start, end):
        def one(q, _):
            late_rows(q)
            return 0

        lax.fori_loop(start, end, one, 0)

    def early_rows(q):
        @pl.when(tm > 0)
        def _():
            halo_copy(q).wait_recv()

        block = jnp.concatenate([halo[q], slab[q, :REACH, :]], axis=0)
        white[q, :REACH, :] = white[q, :REACH, :] + filtered(block)

    def subtract(q):
        high, low = split(coeffs[q])
        white[q] = white[q] - stacked_product(basis_split[...], high, low)

    def piece(half, p):
        return wide.at[half, pl.ds(PIECE_ORDER[p] * PIECE_ROWS, PIECE_ROWS), :]

    def flow(half, p):
        y_to = (y + 1) % ny if half == 0 else (y + ny - 1) % ny
        return send(
            piece(half, p), piece(half, p), flow_send.at[half, p], flow_recv.at[half, p],
            at(coef_to=y_to * 2),
        )

    def to_core(half, p):
        return send(
            piece(half, p), piece(half, p), core_send.at[half, p], core_recv.at[half, p],
            at(coef_to=y * 2 + 1),
        )

    end_of = (ny - 1, 1)
    own_pieces = 4

    @pl.when(is_source)
    def _():
        for p in range(own_pieces):
            for half in range(2):
                flow(half, p).start()
                to_core(half, p).start()

    build_bands(taps_ref, ahead, behind, behind_split)
    for q in range(CHUNKS):
        pltpu.make_async_copy(
            design.at[:, pl.ds(q * CHUNK, CHUNK)], slab.at[q], load_sem.at[q]
        ).wait()
    start_halo(FIRST, (0, 1), (3, 4), ())

    @pl.when(core == 1)
    def _():
        late_range(0, CHUNKS)

    for p in range(PIECES):
        if own_pieces <= p < PIECES:

            @pl.when(is_source)
            def _():
                direction, part = p % 2, (p - own_pieces) // 2

                @pl.when((tm > 0) if direction == 0 else (tm < last_tm))
                def _():
                    for half in range(2):
                        side(direction, half, part).wait_recv()

                for half in range(2):
                    flow(half, p).start()
                    to_core(half, p).start()

        for half in range(2):

            @pl.when((core == 0) & (y != end_of[half]) & (y != 0))
            def _():
                flow(half, p).wait_recv()
                flow(half, p).start()
                to_core(half, p).start()

    for half in range(2):

        @pl.when((core == 0) & (y == end_of[half]))
        def _():
            for p in range(PIECES):
                flow(half, p).wait_recv()
                to_core(half, p).start()

    @pl.when(core == 1)
    def _():
        for p in range(PIECES):
            for half in range(2):
                to_core(half, p).wait_recv()

    def panel_tile(i):
        rows = pl.ds(i * TILE, 4 * TILE)
        window = jnp.concatenate([wide[0, rows, :], wide[1, rows, :]], axis=1)
        return exact(behind[...], window)

    for i in range(ROWS // TILE):
        panel[i * TILE : (i + 1) * TILE, :] = panel_tile(i)
    own_panel = panel[:ROWS, :]
    work[:, :PANEL] = exact(own_panel.T, own_panel)
    for j in range(nz):
        rows = pl.ds(pl.multiple_of(coef * 32 + (j // 2) * 8, 8), 8)
        gram_own[j] = work[rows, (j % 2) * TILE : (j % 2 + 1) * TILE]

    def gram_scatter(d):
        return send(
            gram_own.at[(z + d) % nz], gram_in.at[z], gz_send.at[d], gz_recv.at[z],
            at(z_to=(z + d) % nz),
        )

    def gram_scatter_in(d):
        peer = (z + d) % nz
        return send(gram_own.at[peer], gram_in.at[peer], gz_send.at[d], gz_recv.at[peer], at(z_to=peer))

    def gram_across(step):
        part = gram_x.at[(x + step) % NX]
        return send(part, part, gx_send.at[step], gx_recv.at[step], at(x_to=(x + NX - 1) % NX))

    def gram_across_in(step):
        part = gram_x.at[(x + step + 1) % NX]
        return send(part, part, gx_send.at[step], gx_recv.at[step], at(x_to=(x + 1) % NX))

    def gram_gather(d):
        part = gram_all.at[coef, z]
        return send(part, part, ga_send.at[d], ga_recv.at[z], at(z_to=(z + d) % nz))

    def gram_gather_in(d):
        peer = (z + d) % nz
        part = gram_all.at[coef, peer]
        return send(part, part, ga_send.at[d], ga_recv.at[peer], at(z_to=peer))

    def gram_spread(d):
        part = gram_all.at[coef]
        return send(part, part, gc_send.at[d], gc_recv.at[coef], at(coef_to=(coef + d) % (2 * ny)))

    def gram_spread_in(d):
        peer = (coef + d) % (2 * ny)
        part = gram_all.at[peer]
        return send(part, part, gc_send.at[d], gc_recv.at[peer], at(coef_to=peer))

    for d in range(1, nz):
        gram_scatter(d).start()
    start_halo((), (), (), (3, 4))

    for i in range(ROWS // TILE, (ROWS + REACH) // TILE):
        panel[i * TILE : (i + 1) * TILE, :] = jnp.where(tm == last_tm, 0.0, panel_tile(i))
    for i in range(ROWS // TILE):
        columns = slice(i * TILE, (i + 1) * TILE)
        tile = exact(ahead[...], panel[i * TILE : i * TILE + 4 * TILE, :])
        high, low = split(tile.T)
        cross_left[:PANEL, columns] = high
        cross_left[PANEL:, columns] = low

    def cross_chunk(q):
        high, low = split(slab[q])
        crossed[q] = stacked_product(cross_left[...], high, low)

    def sub(s):
        return pl.ds(s * SUB_ROWS, SUB_ROWS)

    def up_index(step):
        return (z + PLUS - step) % nz

    def down_index(step):
        return (z + nz - MINUS + step) % nz

    def reduce_up(step, s):
        return send(
            crossed.at[up_index(step), sub(s), :], from_minus.at[step, sub(s), :],
            rp_send.at[step, s], rp_recv.at[step, s], at(z_to=(z + 1) % nz),
        )

    def reduce_down(step, s):
        return send(
            crossed.at[down_index(step), sub(s), :], from_plus.at[step, sub(s), :],
            rm_send.at[step, s], rm_recv.at[step, s], at(z_to=(z + nz - 1) % nz),
        )

    def start_sums(kind):
        for s in range(SUBS):
            kind(0, s).start()

    def pass_up(step):
        for s in range(SUBS):
            reduce_up(step - 1, s).wait_recv()
            index = up_index(step)
            crossed[index, sub(s), :] = crossed[index, sub(s), :] + from_minus[step - 1, sub(s), :]
            if step < PLUS:
                reduce_up(step, s).start()

    def pass_down(step):
        for s in range(SUBS):
            reduce_down(step - 1, s).wait_recv()
            index = down_index(step)
            crossed[index, sub(s), :] = crossed[index, sub(s), :] + from_plus[step - 1, sub(s), :]
            if step < MINUS:
                reduce_down(step, s).start()

    cross_chunk(down_index(0))
    start_sums(reduce_down)
    cross_chunk(up_index(0))
    start_sums(reduce_up)

    total = gram_own[z]
    for d in range(1, nz):
        gram_scatter_in(d).wait_recv()
        total = total + gram_in[(z + d) % nz]
    gram_x[x] = total
    gram_across(0).start()
    cross_chunk(down_index(1))
    cross_chunk(up_index(1))
    cross_chunk(down_index(2))
    cross_chunk(up_index(2))
    gram_across_in(0).wait_recv()
    gram_across(1).start()
    cross_chunk(down_index(3))
    cross_chunk(z)

    gram_across_in(1).wait_recv()
    gram_across(2).start()
    pass_down(1)
    pass_up(1)
    gram_across_in(2).wait_recv()
    total = gram_x[0]
    for i in range(1, NX):
        total = total + gram_x[i]
    gram_all[coef, z] = total
    for d in range(1, nz):
        gram_gather(d).start()

    @pl.when(core == 0)
    def _():
        late_range(0, CHUNKS // 2)

    for d in range(1, nz):
        gram_gather_in(d).wait_recv()
    for d in range(1, 2 * ny):
        gram_spread(d).start()

    @pl.when(core == 0)
    def _():
        late_range(CHUNKS // 2, CHUNKS)

    for d in range(1, 2 * ny):
        gram_spread_in(d).wait_recv()
    for c in range(2 * ny):
        for j in range(nz):
            top = c * 32 + (j // 2) * 8
            work[top : top + 8, (j % 2) * TILE : (j % 2 + 1) * TILE] = gram_all[c, j]
    eye_row = lax.broadcasted_iota(jnp.int32, (PANEL, PANEL), 0)
    eye_column = lax.broadcasted_iota(jnp.int32, (PANEL, PANEL), 1)
    work[:, PANEL:] = jnp.where(eye_row == eye_column, 1.0, 0.0).astype(F32)

    pass_down(2)
    pass_up(2)
    start_halo((), (2,), (5, 7), ())
    eliminate(work, 0)
    pass_down(3)
    pass_up(3)
    eliminate(work, 1)
    pass_down(4)

    quarter = PANEL // NX

    def x_rows(index):
        return pl.ds(pl.multiple_of(index * quarter, quarter), quarter)

    def across_out(d):
        peer = (x + d) % NX
        return send(
            crossed.at[z, x_rows(peer), :], across.at[x], xs_send.at[d], xs_recv.at[x],
            at(x_to=peer),
        )

    def across_in(d):
        peer = (x + d) % NX
        return send(
            crossed.at[z, x_rows(peer), :], across.at[peer], xs_send.at[d], xs_recv.at[peer],
            at(x_to=peer),
        )

    def gather_out(d):
        part = gathered.at[x_rows(x), :]
        return send(part, part, xg_send.at[d], xg_recv.at[x], at(x_to=(x + d) % NX))

    def gather_in(d):
        peer = (x + d) % NX
        part = gathered.at[x_rows(peer), :]
        return send(part, part, xg_send.at[d], xg_recv.at[peer], at(x_to=peer))

    for d in range(1, NX):
        across_out(d).start()
    eliminate(work, 2)
    total = crossed[z, x_rows(x), :]
    for d in range(1, NX):
        across_in(d).wait_recv()
        total = total + across[(x + d) % NX]
    gathered[x_rows(x), :] = total
    for d in range(1, NX):
        gather_out(d).start()
    eliminate(work, 3)
    for d in range(1, NX):
        gather_in(d).wait_recv()
    coeffs[z] = exact(work[:, PANEL:], gathered[...])

    def ring_up(step, s):
        part = coeffs.at[(z + nz - step) % nz, sub(s), :]
        return send(part, part, ap_send.at[step, s], ap_recv.at[step, s], at(z_to=(z + 1) % nz))

    def ring_up_in(step, s):
        part = coeffs.at[(z + nz - step) % nz, sub(s), :]
        return send(part, part, ap_send.at[step - 1, s], ap_recv.at[step - 1, s], at(z_to=(z + 1) % nz))

    def ring_down(step, s):
        part = coeffs.at[(z + step) % nz, sub(s), :]
        return send(part, part, am_send.at[step, s], am_recv.at[step, s], at(z_to=(z + nz - 1) % nz))

    def ring_down_in(step, s):
        part = coeffs.at[(z + step) % nz, sub(s), :]
        return send(part, part, am_send.at[step - 1, s], am_recv.at[step - 1, s], at(z_to=(z + 1) % nz))

    up_hops, down_hops = PLUS, MINUS
    for s in range(SUBS):
        ring_up(0, s).start()
        ring_down(0, s).start()
    start_halo(LAST, (6,), (), (5, 7))
    basis[...] = exact(panel[:ROWS, :], work[:, PANEL:].T)
    high, low = split(basis[...])
    basis_split[:ROWS, :] = high
    basis_split[ROWS:, :] = low
    subtract(z)
    for q in (0, 1, 3, 4, 2):
        early_rows(q)
    after = ((), (5,), (6,), (7,))
    for step in range(1, max(up_hops, down_hops) + 1):
        for s in range(SUBS):
            if step <= down_hops:
                ring_down_in(step, s).wait_recv()
                if step < down_hops:
                    ring_down(step, s).start()
            if step <= up_hops:
                ring_up_in(step, s).wait_recv()
                if step < up_hops:
                    ring_up(step, s).start()
        if step <= up_hops:
            subtract((z + nz - step) % nz)
        for q in after[step - 1]:
            early_rows(q)
        if step <= down_hops:
            subtract((z + step) % nz)

    @pl.when(is_source)
    def _():
        white[0] = basis[...] * float((nz * NX * ROWS) ** 0.5)

    @pl.when(x < NX - 1)
    def _():
        for q in range(CHUNKS):
            halo_copy(q).wait_send()

    @pl.when(wrap_up)
    def _():
        for q in range(CHUNKS):
            if q in RELAYED:
                relay_out(q).wait_send()
            else:
                halo_copy(q).wait_send()

    @pl.when(wrap_relay)
    def _():
        for q in RELAYED:
            relay_on(q).wait_send()

    @pl.when(is_source)
    def _():
        for direction in range(2):

            @pl.when((tm < last_tm) if direction == 0 else (tm > 0))
            def _():
                for part in range(2):
                    for half in range(2):
                        side(direction, half, part).wait_send()

    @pl.when(core == 0)
    def _():
        for half in range(2):
            for p in range(PIECES):
                to_core(half, p).wait_send()

            @pl.when(y != end_of[half])
            def _():
                for p in range(PIECES):
                    flow(half, p).wait_send()

    for d in range(1, nz):
        gram_scatter(d).wait_send()
        gram_gather(d).wait_send()
    for d in range(1, NX):
        gram_across(d - 1).wait_send()
        across_out(d).wait_send()
        gather_out(d).wait_send()
    for d in range(1, 2 * ny):
        gram_spread(d).wait_send()
    for s in range(SUBS):
        for step in range(PLUS):
            reduce_up(step, s).wait_send()
        for step in range(MINUS):
            reduce_down(step, s).wait_send()
        for step in range(up_hops):
            ring_up(step, s).wait_send()
        for step in range(down_hops):
            ring_down(step, s).wait_send()


def finish_kernel(white, coeffs, coeffs_out, reduced_out, sems):
    copies = []
    for q in range(CHUNKS):
        columns = pl.ds(q * CHUNK, CHUNK)
        copies.append(pltpu.make_async_copy(white.at[q], reduced_out.at[:, columns], sems.at[0, q]))
        copies.append(pltpu.make_async_copy(coeffs.at[q], coeffs_out.at[:, columns], sems.at[1, q]))
    for copy in copies:
        copy.start()
    for copy in copies:
        copy.wait()


def per_device(nz, ny, design, taps):
    dma = pltpu.SemaphoreType.DMA
    vmem = pltpu.VMEM
    white, coeffs = pl.pallas_call(
        functools.partial(exchange_kernel, nz, ny),
        out_shape=(
            vmem((CHUNKS, ROWS, CHUNK), F32),
            vmem((CHUNKS, PANEL, CHUNK), F32),
        ),
        in_specs=[pl.BlockSpec(memory_space=pltpu.VMEM), pl.BlockSpec(memory_space=pl.ANY)],
        out_specs=[pl.BlockSpec(memory_space=pltpu.VMEM)] * 2,
        scratch_shapes=[
            vmem((ROWS, PANEL), F32),
            vmem((2 * ROWS, PANEL), BF16),
            vmem((CHUNKS, ROWS, CHUNK), F32),
            vmem((CHUNKS, REACH, CHUNK), F32),
            vmem((len(RELAYED), REACH, CHUNK), F32),
            vmem((2, 2 * REACH + ROWS, TILE), F32),
            vmem((ROWS + REACH, PANEL), F32),
            vmem((2 * PANEL, ROWS), BF16),
            vmem((TILE, 4 * TILE), F32),
            vmem((TILE, 4 * TILE), F32),
            vmem((2 * TILE, 4 * TILE), BF16),
            vmem((CHUNKS, PANEL, CHUNK), F32),
            vmem((PLUS, PANEL, CHUNK), F32),
            vmem((MINUS, PANEL, CHUNK), F32),
            vmem((NX, PANEL // NX, CHUNK), F32),
            vmem((PANEL, CHUNK), F32),
            vmem((nz, 8, TILE), F32),
            vmem((nz, 8, TILE), F32),
            vmem((NX, 8, TILE), F32),
            vmem((2 * ny, nz, 8, TILE), F32),
            vmem((PANEL, 2 * PANEL), F32),
            dma((CHUNKS,)), dma((CHUNKS,)), dma((CHUNKS,)),
            dma((2, len(RELAYED))), dma((len(RELAYED),)),
            dma((2, 2, 2)), dma((2, 2, 2)), dma((2,)),
            dma((2, PIECES)), dma((2, PIECES)), dma((2, PIECES)), dma((2, PIECES)),
            dma((nz,)), dma((nz,)), dma((NX,)), dma((NX,)),
            dma((nz,)), dma((nz,)), dma((2 * ny,)), dma((2 * ny,)),
            dma((PLUS, SUBS)), dma((PLUS, SUBS)), dma((MINUS, SUBS)), dma((MINUS, SUBS)),
            dma((NX,)), dma((NX,)), dma((NX,)), dma((NX,)),
            dma((PLUS, SUBS)), dma((PLUS, SUBS)), dma((MINUS, SUBS)), dma((MINUS, SUBS)),
        ],
        compiler_params=pltpu.CompilerParams(
            collective_id=0, has_side_effects=True, vmem_limit_bytes=40 * 1024 * 1024
        ),
    )(taps.reshape(1, -1), design)
    keep = pltpu.with_memory_space_constraint
    return pl.pallas_call(
        finish_kernel,
        out_shape=(
            jax.ShapeDtypeStruct((PANEL, COLUMNS), F32),
            jax.ShapeDtypeStruct((ROWS, COLUMNS), F32),
        ),
        in_specs=[pl.BlockSpec(memory_space=pltpu.VMEM)] * 2,
        out_specs=[pl.BlockSpec(memory_space=pl.ANY)] * 2,
        scratch_shapes=[dma((2, CHUNKS))],
        compiler_params=pltpu.CompilerParams(vmem_limit_bytes=8 * 1024 * 1024),
    )(keep(white, pltpu.VMEM), keep(coeffs, pltpu.VMEM))


def solution(mesh):
    nz = mesh.shape["tm"] // NX
    ny = mesh.shape["coef"] // 2
    in_specs = (P("tm", "coef"), P())
    out_specs = (P(None, "coef"), P("tm", "coef"))
    return jax.shard_map(
        functools.partial(per_device, nz, ny), mesh=mesh, in_specs=in_specs,
        out_specs=out_specs, check_vma=False,
    )
```

```python
import functools

import jax
import jax.numpy as jnp
from jax import lax
from jax.experimental import pallas as pl
from jax.experimental.pallas import tpu as pltpu
from jax.sharding import PartitionSpec as P

MESH = pl.DeviceIdType.MESH
F32 = jnp.float32
BF16 = jnp.bfloat16
HIGHEST = lax.Precision.HIGHEST
PANEL = 256
ROWS = 768
REACH = 384
COLUMNS = 2048
CHUNK = 256
CHUNKS = COLUMNS // CHUNK
TILE = 128
NX = 4
PIECES = 8
PIECE_ROWS = 192
PIECE_ORDER = (2, 3, 4, 5, 0, 6, 1, 7)
PLUS = 3
MINUS = 4
SUBS = 2
SUB_ROWS = PANEL // SUBS
FIRST, LAST = (0, 1, 2, 3, 4, 5), (6, 7)
RELAYED = (3, 4, 5, 7)


def split(value):
    high = value.astype(BF16)
    low = (value - high.astype(F32)).astype(BF16)
    return high, low


def dot(left, right):
    return jnp.dot(left, right, preferred_element_type=F32)


def exact(left, right):
    return jnp.dot(left, right, precision=HIGHEST, preferred_element_type=F32)


def stacked_product(stacked, high, low):
    rows = stacked.shape[0] // 2
    both = dot(stacked, high)
    return both[:rows] + (both[rows:] + dot(stacked[:rows], low))


def build_bands(taps_ref, ahead, behind, behind_split):
    line = jnp.concatenate([taps_ref[...], jnp.zeros((1, TILE), F32)], axis=1)
    band = jnp.broadcast_to(line, (TILE, 4 * TILE))
    row = lax.broadcasted_iota(jnp.int32, (TILE, 4 * TILE), 0)
    step = 1
    while step < TILE:
        band = jnp.where((row // step) % 2 == 1, pltpu.roll(band, step, 1), band)
        step *= 2
    ahead[...] = band
    for block in range(4):
        part = band[:, (3 - block) * TILE : (4 - block) * TILE].T
        columns = slice(block * TILE, (block + 1) * TILE)
        behind[:, columns] = part
        high, low = split(part)
        behind_split[:TILE, columns] = high
        behind_split[TILE:, columns] = low


def eliminate(work, block):
    size = 64
    top = block * size
    rows = slice(top, top + size)
    square = work[rows, top : top + size]
    eye_row = lax.broadcasted_iota(jnp.int32, (size, size), 0)
    eye_column = lax.broadcasted_iota(jnp.int32, (size, size), 1)
    eye = jnp.where(eye_row == eye_column, 1.0, 0.0).astype(F32)
    table = jnp.concatenate([square, eye], axis=1)
    row = lax.broadcasted_iota(jnp.int32, (size, 2 * size), 0)
    for j in range(size):
        column = jnp.broadcast_to(table[:, j : j + 1], (size, 2 * size))
        inverse_root = lax.rsqrt(column[j : j + 1, :])
        pivot = table[j : j + 1, :] * inverse_root
        factor = column * inverse_root
        table = jnp.where(row == j, pivot, jnp.where(row > j, table - factor * pivot, table))
    inverse = table[:, size:]
    panel_rows = exact(inverse, work[rows, :])
    work[rows, :] = panel_rows
    if top + size < PANEL:
        left = panel_rows[:, :PANEL].T[top + size :]
        rest = slice(top + size, PANEL)
        work[rest, :] = work[rest, :] - exact(left, panel_rows)


def exchange_kernel(
    nz, ny, taps_ref, design, white, coeffs,
    basis, basis_split, slab, halo, relay, wide, panel, cross_left, ahead, behind, behind_split, crossed,
    from_minus, from_plus, across, gathered, gram_own, gram_in, gram_x, gram_all, work,
    load_sem, halo_send, halo_recv, relay_send, relay_recv, side_send, side_recv, own_sem,
    flow_send, flow_recv, core_send, core_recv,
    gz_send, gz_recv, gx_send, gx_recv, ga_send, ga_recv, gc_send, gc_recv,
    rp_send, rp_recv, rm_send, rm_recv, xs_send, xs_recv, xg_send, xg_recv,
    ap_send, ap_recv, am_send, am_recv,
):
    tm = lax.axis_index("tm")
    coef = lax.axis_index("coef")
    last_tm = nz * NX - 1
    z, x = tm // NX, tm % NX
    y, core = coef // 2, coef % 2
    is_source = coef == 0

    def at(z_to=z, x_to=x, coef_to=coef):
        return (z_to * NX + x_to, coef_to)

    def send(source, target, send_sem, recv_sem, device):
        return pltpu.make_async_remote_copy(
            src_ref=source, dst_ref=target, send_sem=send_sem, recv_sem=recv_sem,
            device_id=device, device_id_type=MESH,
        )

    wrap_up = (x == NX - 1) & (tm < last_tm)
    wrap_down = (x == 0) & (tm > 0)

    def own(half):
        return pltpu.make_async_copy(
            design.at[:, pl.ds(half * TILE, TILE)],
            wide.at[half, pl.ds(REACH, ROWS), :],
            own_sem.at[half],
        )

    @pl.when(is_source)
    def _():
        for half in range(2):
            own(half).start()

    for q in range(CHUNKS):
        pltpu.make_async_copy(
            design.at[:, pl.ds(q * CHUNK, CHUNK)], slab.at[q], load_sem.at[q]
        ).start()

    barrier = pltpu.get_barrier_semaphore()

    def greet(device):
        pl.semaphore_signal(barrier, inc=1, device_id=device, device_id_type=MESH)

    for d in range(1, nz):
        greet(at(z_to=(z + d) % nz))
    for d in range(1, NX):
        greet(at(x_to=(x + d) % NX))
    for d in range(1, 2 * ny):
        greet(at(coef_to=(coef + d) % (2 * ny)))
    greetings = nz - 1 + NX - 1 + 2 * ny - 1

    @pl.when(wrap_up)
    def _():
        greet((tm + 1, coef))

    @pl.when(wrap_down)
    def _():
        greet((tm - 1, coef))

    extra = jnp.where(wrap_up, 1, 0) + jnp.where(wrap_down, 1, 0)
    pl.semaphore_wait(barrier, greetings + extra)

    def side(direction, half, part):
        skip = part * PIECE_ROWS
        if direction == 0:
            source = wide.at[half, pl.ds(ROWS + skip, PIECE_ROWS), :]
            device, start = (tm + 1, coef), skip
        else:
            source = wide.at[half, pl.ds(REACH + skip, PIECE_ROWS), :]
            device, start = (tm - 1, coef), REACH + ROWS + skip
        target = wide.at[half, pl.ds(start, PIECE_ROWS), :]
        sems = side_send.at[direction, half, part], side_recv.at[direction, half, part]
        return send(source, target, *sems, device)

    def halo_source(q):
        return slab.at[q, pl.ds(ROWS - REACH, REACH), :]

    def halo_copy(q):
        sems = halo_send.at[q], halo_recv.at[q]
        return send(halo_source(q), halo.at[q], *sems, (tm + 1, coef))

    def relay_out(q):
        i = RELAYED.index(q)
        sems = relay_send.at[0, i], relay_recv.at[i]
        return send(halo_source(q), relay.at[i], *sems, at(z_to=(z + 1) % nz))

    def relay_on(q):
        i = RELAYED.index(q)
        sems = relay_send.at[1, i], halo_recv.at[q]
        return send(relay.at[i], halo.at[q], *sems, at(x_to=(x + 1) % NX))

    wrap_relay = (x == NX - 1) & (z > 0)

    def start_halo(group, direct, relayed, passed):
        if group:

            @pl.when(x < NX - 1)
            def _():
                for q in group:
                    halo_copy(q).start()

        if relayed:

            @pl.when(wrap_up)
            def _():
                for q in relayed:
                    relay_out(q).start()

        if direct or passed:

            @pl.when(x == NX - 1)
            def _():
                for q in sorted(direct + passed):
                    if q in passed:

                        @pl.when(z > 0)
                        def _():
                            relay_out(q).wait_recv()
                            relay_on(q).start()

                    else:

                        @pl.when(tm < last_tm)
                        def _():
                            halo_copy(q).start()

    @pl.when(is_source)
    def _():
        for half in range(2):
            own(half).wait()

        @pl.when(tm < last_tm)
        def _():
            for part in range(2):
                for half in range(2):
                    side(0, half, part).start()

        @pl.when(tm > 0)
        def _():
            for part in range(2):
                for half in range(2):
                    side(1, half, part).start()

        @pl.when(tm == 0)
        def _():
            wide[:, :REACH, :] = jnp.zeros((2, REACH, TILE), F32)

        @pl.when(tm == last_tm)
        def _():
            wide[:, REACH + ROWS :, :] = jnp.zeros((2, REACH, TILE), F32)

    @pl.when(tm == 0)
    def _():
        for q in range(CHUNKS):
            halo[q] = jnp.zeros((REACH, CHUNK), F32)

    def filtered(block):
        high, low = split(block)
        parts = []
        for i in range(3):
            window = slice(i * TILE, i * TILE + 4 * TILE)
            parts.append(stacked_product(behind_split[...], high[window], low[window]))
        return jnp.concatenate(parts, axis=0)

    def late_rows(q):
        white[q, REACH:, :] = filtered(slab[q])
        white[q, :REACH, :] = jnp.zeros((REACH, CHUNK), F32)

    def late_range(start, end):
        def one(q, _):
            late_rows(q)
            return 0

        lax.fori_loop(start, end, one, 0)

    def early_rows(q):
        @pl.when(tm > 0)
        def _():
            halo_copy(q).wait_recv()

        block = jnp.concatenate([halo[q], slab[q, :REACH, :]], axis=0)
        white[q, :REACH, :] = white[q, :REACH, :] + filtered(block)

    def subtract(q):
        high, low = split(coeffs[q])
        white[q] = white[q] - stacked_product(basis_split[...], high, low)

    def piece(half, p):
        return wide.at[half, pl.ds(PIECE_ORDER[p] * PIECE_ROWS, PIECE_ROWS), :]

    def flow(half, p):
        y_to = (y + 1) % ny if half == 0 else (y + ny - 1) % ny
        return send(
            piece(half, p), piece(half, p), flow_send.at[half, p], flow_recv.at[half, p],
            at(coef_to=y_to * 2),
        )

    def to_core(half, p):
        return send(
            piece(half, p), piece(half, p), core_send.at[half, p], core_recv.at[half, p],
            at(coef_to=y * 2 + 1),
        )

    end_of = (ny - 1, 1)
    own_pieces = 4

    @pl.when(is_source)
    def _():
        for p in range(own_pieces):
            for half in range(2):
                flow(half, p).start()
                to_core(half, p).start()

    build_bands(taps_ref, ahead, behind, behind_split)
    for q in range(CHUNKS):
        pltpu.make_async_copy(
            design.at[:, pl.ds(q * CHUNK, CHUNK)], slab.at[q], load_sem.at[q]
        ).wait()
    start_halo(FIRST, (0,), (3, 4), ())

    @pl.when(core == 1)
    def _():
        late_range(0, CHUNKS)

    for p in range(PIECES):
        if own_pieces <= p < PIECES:

            @pl.when(is_source)
            def _():
                direction, part = p % 2, (p - own_pieces) // 2

                @pl.when((tm > 0) if direction == 0 else (tm < last_tm))
                def _():
                    for half in range(2):
                        side(direction, half, part).wait_recv()

                for half in range(2):
                    flow(half, p).start()
                    to_core(half, p).start()

        for half in range(2):

            @pl.when((core == 0) & (y != end_of[half]) & (y != 0))
            def _():
                flow(half, p).wait_recv()
                flow(half, p).start()
                to_core(half, p).start()

    for half in range(2):

        @pl.when((core == 0) & (y == end_of[half]))
        def _():
            for p in range(PIECES):
                flow(half, p).wait_recv()
                to_core(half, p).start()

    @pl.when(core == 1)
    def _():
        for p in range(PIECES):
            for half in range(2):
                to_core(half, p).wait_recv()

    def panel_tile(i):
        rows = pl.ds(i * TILE, 4 * TILE)
        window = jnp.concatenate([wide[0, rows, :], wide[1, rows, :]], axis=1)
        return exact(behind[...], window)

    for i in range(ROWS // TILE):
        panel[i * TILE : (i + 1) * TILE, :] = panel_tile(i)
    own_panel = panel[:ROWS, :]
    work[:, :PANEL] = exact(own_panel.T, own_panel)
    for j in range(nz):
        rows = pl.ds(pl.multiple_of(coef * 32 + (j // 2) * 8, 8), 8)
        gram_own[j] = work[rows, (j % 2) * TILE : (j % 2 + 1) * TILE]

    def gram_scatter(d):
        return send(
            gram_own.at[(z + d) % nz], gram_in.at[z], gz_send.at[d], gz_recv.at[z],
            at(z_to=(z + d) % nz),
        )

    def gram_scatter_in(d):
        peer = (z + d) % nz
        return send(gram_own.at[peer], gram_in.at[peer], gz_send.at[d], gz_recv.at[peer], at(z_to=peer))

    def gram_across(step):
        part = gram_x.at[(x + step) % NX]
        return send(part, part, gx_send.at[step], gx_recv.at[step], at(x_to=(x + NX - 1) % NX))

    def gram_across_in(step):
        part = gram_x.at[(x + step + 1) % NX]
        return send(part, part, gx_send.at[step], gx_recv.at[step], at(x_to=(x + 1) % NX))

    def gram_gather(d):
        part = gram_all.at[coef, z]
        return send(part, part, ga_send.at[d], ga_recv.at[z], at(z_to=(z + d) % nz))

    def gram_gather_in(d):
        peer = (z + d) % nz
        part = gram_all.at[coef, peer]
        return send(part, part, ga_send.at[d], ga_recv.at[peer], at(z_to=peer))

    def gram_spread(d):
        part = gram_all.at[coef]
        return send(part, part, gc_send.at[d], gc_recv.at[coef], at(coef_to=(coef + d) % (2 * ny)))

    def gram_spread_in(d):
        peer = (coef + d) % (2 * ny)
        part = gram_all.at[peer]
        return send(part, part, gc_send.at[d], gc_recv.at[peer], at(coef_to=peer))

    for d in range(1, nz):
        gram_scatter(d).start()
    start_halo((), (), (), (3, 4))

    for i in range(ROWS // TILE, (ROWS + REACH) // TILE):
        panel[i * TILE : (i + 1) * TILE, :] = jnp.where(tm == last_tm, 0.0, panel_tile(i))
    for i in range(ROWS // TILE):
        columns = slice(i * TILE, (i + 1) * TILE)
        tile = exact(ahead[...], panel[i * TILE : i * TILE + 4 * TILE, :])
        high, low = split(tile.T)
        cross_left[:PANEL, columns] = high
        cross_left[PANEL:, columns] = low

    def cross_chunk(q):
        high, low = split(slab[q])
        crossed[q] = stacked_product(cross_left[...], high, low)

    def sub(s):
        return pl.ds(s * SUB_ROWS, SUB_ROWS)

    def up_index(step):
        return (z + PLUS - step) % nz

    def down_index(step):
        return (z + nz - MINUS + step) % nz

    def reduce_up(step, s):
        return send(
            crossed.at[up_index(step), sub(s), :], from_minus.at[step, sub(s), :],
            rp_send.at[step, s], rp_recv.at[step, s], at(z_to=(z + 1) % nz),
        )

    def reduce_down(step, s):
        return send(
            crossed.at[down_index(step), sub(s), :], from_plus.at[step, sub(s), :],
            rm_send.at[step, s], rm_recv.at[step, s], at(z_to=(z + nz - 1) % nz),
        )

    def start_sums(kind):
        for s in range(SUBS):
            kind(0, s).start()

    def pass_up(step):
        for s in range(SUBS):
            reduce_up(step - 1, s).wait_recv()
            index = up_index(step)
            crossed[index, sub(s), :] = crossed[index, sub(s), :] + from_minus[step - 1, sub(s), :]
            if step < PLUS:
                reduce_up(step, s).start()

    def pass_down(step):
        for s in range(SUBS):
            reduce_down(step - 1, s).wait_recv()
            index = down_index(step)
            crossed[index, sub(s), :] = crossed[index, sub(s), :] + from_plus[step - 1, sub(s), :]
            if step < MINUS:
                reduce_down(step, s).start()

    cross_chunk(down_index(0))
    start_sums(reduce_down)
    cross_chunk(up_index(0))
    start_sums(reduce_up)

    total = gram_own[z]
    for d in range(1, nz):
        gram_scatter_in(d).wait_recv()
        total = total + gram_in[(z + d) % nz]
    gram_x[x] = total
    gram_across(0).start()
    cross_chunk(down_index(1))
    cross_chunk(up_index(1))
    cross_chunk(down_index(2))
    cross_chunk(up_index(2))
    gram_across_in(0).wait_recv()
    gram_across(1).start()
    cross_chunk(down_index(3))
    cross_chunk(z)

    gram_across_in(1).wait_recv()
    gram_across(2).start()
    pass_down(1)
    pass_up(1)
    gram_across_in(2).wait_recv()
    total = gram_x[0]
    for i in range(1, NX):
        total = total + gram_x[i]
    gram_all[coef, z] = total
    for d in range(1, nz):
        gram_gather(d).start()

    @pl.when(core == 0)
    def _():
        late_range(0, CHUNKS // 2)

    for d in range(1, nz):
        gram_gather_in(d).wait_recv()
    for d in range(1, 2 * ny):
        gram_spread(d).start()

    @pl.when(core == 0)
    def _():
        late_range(CHUNKS // 2, CHUNKS)

    for d in range(1, 2 * ny):
        gram_spread_in(d).wait_recv()
    for c in range(2 * ny):
        for j in range(nz):
            top = c * 32 + (j // 2) * 8
            work[top : top + 8, (j % 2) * TILE : (j % 2 + 1) * TILE] = gram_all[c, j]
    eye_row = lax.broadcasted_iota(jnp.int32, (PANEL, PANEL), 0)
    eye_column = lax.broadcasted_iota(jnp.int32, (PANEL, PANEL), 1)
    work[:, PANEL:] = jnp.where(eye_row == eye_column, 1.0, 0.0).astype(F32)

    pass_down(2)
    pass_up(2)
    start_halo((), (1, 2), (5, 7), ())
    eliminate(work, 0)
    pass_down(3)
    pass_up(3)
    eliminate(work, 1)
    pass_down(4)

    quarter = PANEL // NX

    def x_rows(index):
        return pl.ds(pl.multiple_of(index * quarter, quarter), quarter)

    def across_out(d):
        peer = (x + d) % NX
        return send(
            crossed.at[z, x_rows(peer), :], across.at[x], xs_send.at[d], xs_recv.at[x],
            at(x_to=peer),
        )

    def across_in(d):
        peer = (x + d) % NX
        return send(
            crossed.at[z, x_rows(peer), :], across.at[peer], xs_send.at[d], xs_recv.at[peer],
            at(x_to=peer),
        )

    def gather_out(d):
        part = gathered.at[x_rows(x), :]
        return send(part, part, xg_send.at[d], xg_recv.at[x], at(x_to=(x + d) % NX))

    def gather_in(d):
        peer = (x + d) % NX
        part = gathered.at[x_rows(peer), :]
        return send(part, part, xg_send.at[d], xg_recv.at[peer], at(x_to=peer))

    for d in range(1, NX):
        across_out(d).start()
    eliminate(work, 2)
    total = crossed[z, x_rows(x), :]
    for d in range(1, NX):
        across_in(d).wait_recv()
        total = total + across[(x + d) % NX]
    gathered[x_rows(x), :] = total
    for d in range(1, NX):
        gather_out(d).start()
    eliminate(work, 3)
    for d in range(1, NX):
        gather_in(d).wait_recv()
    coeffs[z] = exact(work[:, PANEL:], gathered[...])

    def ring_up(step, s):
        part = coeffs.at[(z + nz - step) % nz, sub(s), :]
        return send(part, part, ap_send.at[step, s], ap_recv.at[step, s], at(z_to=(z + 1) % nz))

    def ring_up_in(step, s):
        part = coeffs.at[(z + nz - step) % nz, sub(s), :]
        return send(part, part, ap_send.at[step - 1, s], ap_recv.at[step - 1, s], at(z_to=(z + 1) % nz))

    def ring_down(step, s):
        part = coeffs.at[(z + step) % nz, sub(s), :]
        return send(part, part, am_send.at[step, s], am_recv.at[step, s], at(z_to=(z + nz - 1) % nz))

    def ring_down_in(step, s):
        part = coeffs.at[(z + step) % nz, sub(s), :]
        return send(part, part, am_send.at[step - 1, s], am_recv.at[step - 1, s], at(z_to=(z + 1) % nz))

    up_hops, down_hops = PLUS, MINUS
    for s in range(SUBS):
        ring_up(0, s).start()
        ring_down(0, s).start()
    start_halo(LAST, (6,), (), (5, 7))
    basis[...] = exact(panel[:ROWS, :], work[:, PANEL:].T)
    high, low = split(basis[...])
    basis_split[:ROWS, :] = high
    basis_split[ROWS:, :] = low
    subtract(z)
    for q in (0, 3, 4, 1, 2):
        early_rows(q)
    after = ((), (5,), (6,), (7,))
    for step in range(1, max(up_hops, down_hops) + 1):
        for s in range(SUBS):
            if step <= down_hops:
                ring_down_in(step, s).wait_recv()
                if step < down_hops:
                    ring_down(step, s).start()
            if step <= up_hops:
                ring_up_in(step, s).wait_recv()
                if step < up_hops:
                    ring_up(step, s).start()
        if step <= up_hops:
            subtract((z + nz - step) % nz)
        for q in after[step - 1]:
            early_rows(q)
        if step <= down_hops:
            subtract((z + step) % nz)

    @pl.when(is_source)
    def _():
        white[0] = basis[...] * float((nz * NX * ROWS) ** 0.5)

    @pl.when(x < NX - 1)
    def _():
        for q in range(CHUNKS):
            halo_copy(q).wait_send()

    @pl.when(wrap_up)
    def _():
        for q in range(CHUNKS):
            if q in RELAYED:
                relay_out(q).wait_send()
            else:
                halo_copy(q).wait_send()

    @pl.when(wrap_relay)
    def _():
        for q in RELAYED:
            relay_on(q).wait_send()

    @pl.when(is_source)
    def _():
        for direction in range(2):

            @pl.when((tm < last_tm) if direction == 0 else (tm > 0))
            def _():
                for part in range(2):
                    for half in range(2):
                        side(direction, half, part).wait_send()

    @pl.when(core == 0)
    def _():
        for half in range(2):
            for p in range(PIECES):
                to_core(half, p).wait_send()

            @pl.when(y != end_of[half])
            def _():
                for p in range(PIECES):
                    flow(half, p).wait_send()

    for d in range(1, nz):
        gram_scatter(d).wait_send()
        gram_gather(d).wait_send()
    for d in range(1, NX):
        gram_across(d - 1).wait_send()
        across_out(d).wait_send()
        gather_out(d).wait_send()
    for d in range(1, 2 * ny):
        gram_spread(d).wait_send()
    for s in range(SUBS):
        for step in range(PLUS):
            reduce_up(step, s).wait_send()
        for step in range(MINUS):
            reduce_down(step, s).wait_send()
        for step in range(up_hops):
            ring_up(step, s).wait_send()
        for step in range(down_hops):
            ring_down(step, s).wait_send()


def finish_kernel(white, coeffs, coeffs_out, reduced_out, sems):
    copies = []
    for q in range(CHUNKS):
        columns = pl.ds(q * CHUNK, CHUNK)
        copies.append(pltpu.make_async_copy(white.at[q], reduced_out.at[:, columns], sems.at[0, q]))
        copies.append(pltpu.make_async_copy(coeffs.at[q], coeffs_out.at[:, columns], sems.at[1, q]))
    for copy in copies:
        copy.start()
    for copy in copies:
        copy.wait()


def per_device(nz, ny, design, taps):
    dma = pltpu.SemaphoreType.DMA
    vmem = pltpu.VMEM
    white, coeffs = pl.pallas_call(
        functools.partial(exchange_kernel, nz, ny),
        out_shape=(
            vmem((CHUNKS, ROWS, CHUNK), F32),
            vmem((CHUNKS, PANEL, CHUNK), F32),
        ),
        in_specs=[pl.BlockSpec(memory_space=pltpu.VMEM), pl.BlockSpec(memory_space=pl.ANY)],
        out_specs=[pl.BlockSpec(memory_space=pltpu.VMEM)] * 2,
        scratch_shapes=[
            vmem((ROWS, PANEL), F32),
            vmem((2 * ROWS, PANEL), BF16),
            vmem((CHUNKS, ROWS, CHUNK), F32),
            vmem((CHUNKS, REACH, CHUNK), F32),
            vmem((len(RELAYED), REACH, CHUNK), F32),
            vmem((2, 2 * REACH + ROWS, TILE), F32),
            vmem((ROWS + REACH, PANEL), F32),
            vmem((2 * PANEL, ROWS), BF16),
            vmem((TILE, 4 * TILE), F32),
            vmem((TILE, 4 * TILE), F32),
            vmem((2 * TILE, 4 * TILE), BF16),
            vmem((CHUNKS, PANEL, CHUNK), F32),
            vmem((PLUS, PANEL, CHUNK), F32),
            vmem((MINUS, PANEL, CHUNK), F32),
            vmem((NX, PANEL // NX, CHUNK), F32),
            vmem((PANEL, CHUNK), F32),
            vmem((nz, 8, TILE), F32),
            vmem((nz, 8, TILE), F32),
            vmem((NX, 8, TILE), F32),
            vmem((2 * ny, nz, 8, TILE), F32),
            vmem((PANEL, 2 * PANEL), F32),
            dma((CHUNKS,)), dma((CHUNKS,)), dma((CHUNKS,)),
            dma((2, len(RELAYED))), dma((len(RELAYED),)),
            dma((2, 2, 2)), dma((2, 2, 2)), dma((2,)),
            dma((2, PIECES)), dma((2, PIECES)), dma((2, PIECES)), dma((2, PIECES)),
            dma((nz,)), dma((nz,)), dma((NX,)), dma((NX,)),
            dma((nz,)), dma((nz,)), dma((2 * ny,)), dma((2 * ny,)),
            dma((PLUS, SUBS)), dma((PLUS, SUBS)), dma((MINUS, SUBS)), dma((MINUS, SUBS)),
            dma((NX,)), dma((NX,)), dma((NX,)), dma((NX,)),
            dma((PLUS, SUBS)), dma((PLUS, SUBS)), dma((MINUS, SUBS)), dma((MINUS, SUBS)),
        ],
        compiler_params=pltpu.CompilerParams(
            collective_id=0, has_side_effects=True, vmem_limit_bytes=40 * 1024 * 1024
        ),
    )(taps.reshape(1, -1), design)
    keep = pltpu.with_memory_space_constraint
    return pl.pallas_call(
        finish_kernel,
        out_shape=(
            jax.ShapeDtypeStruct((PANEL, COLUMNS), F32),
            jax.ShapeDtypeStruct((ROWS, COLUMNS), F32),
        ),
        in_specs=[pl.BlockSpec(memory_space=pltpu.VMEM)] * 2,
        out_specs=[pl.BlockSpec(memory_space=pl.ANY)] * 2,
        scratch_shapes=[dma((2, CHUNKS))],
        compiler_params=pltpu.CompilerParams(vmem_limit_bytes=8 * 1024 * 1024),
    )(keep(white, pltpu.VMEM), keep(coeffs, pltpu.VMEM))


def solution(mesh):
    nz = mesh.shape["tm"] // NX
    ny = mesh.shape["coef"] // 2
    in_specs = (P("tm", "coef"), P())
    out_specs = (P(None, "coef"), P("tm", "coef"))
    return jax.shard_map(
        functools.partial(per_device, nz, ny), mesh=mesh, in_specs=in_specs,
        out_specs=out_specs, check_vma=False,
    )
```
